256 devices in a mesh: grp: 8 (over y, core), dev: 32 (over z, x).
Axes of the slice: x: 4, y: 4, z: 8, core: 2. Of those that a mesh axis runs over, the one named last changes fastest.
Arguments:
- signals: float32 [256, 32, 128], P(('grp', 'dev')), may hold values from -6 to 6
- maps: bfloat16 [256, 16, 256, 128], P(('grp', 'dev')), may hold values from -0.01171875 to 0.01171875
- uses: int32 [256, 16], P(('grp', 'dev')), may hold values from 0 to 31, all different within a row; in each aligned block of 32 rows (0 to 31, 32 to 63, ...) at most 20 rows name the same one
- owner: int32 [32], replicated, may hold values from 0 to 31, each once
- local_dict: float32 [8, 32, 64, 32, 256], P('grp', 'dev'), may hold values from -45 to 45
- duals: float32 [8, 32, 64, 32, 256], P('grp', 'dev'), may hold values from -4 to 4
- consensus: float32 [32, 64, 32, 256], P('dev'), may hold values from -6 to 6
Outputs:
- consensus_final: float32 [32, 64, 32, 256], P('dev')
- duals_final: float32 [8, 32, 64, 32, 256], P('grp', 'dev')
- residual: float32 [256, 32, 128], P(('grp', 'dev'))
The draws below stay inside these ranges and needn't reach their ends.
Inputs may be any that keep to these rules, and one draw needn't show every extreme that they name: `uses`: each window names 16 different classes; among the windows of one group at most 20 name one class, and in every draw some class of some group is named by exactly 20 windows. `owner`: each slot holds exactly one class.
All inputs are finite; a program needn't handle non-finite values.
Results may differ from the reference program's by a relative error of at most 0.0053.
Values may be sent and summed in bfloat16 or wider, within the bound.
A program may use at most 128 MiB of HBM per device.

```python
import math
import jax
import jax.numpy as jnp
import numpy as np
from jax import lax

F = 256
C = 32
L = 64
T_SIZE = 128
ITERS = 2
GROUPS = 8
CLASSES = 32
SIGNALS = 256
USES = 16
READERS = 20
N_DEV = 32


def draw_local_dict(key, part):
    key_scale, key_chan, key_base, key_noise = jax.random.split(key, 4)
    low, high = (0.3, 3.0)
    filt_scale = jnp.exp(jax.random.uniform(key_scale, (CLASSES, 1, 1, F), jnp.float32, math.log(low), math.log(high)))
    chan_scale = jnp.exp(jax.random.uniform(key_chan, (CLASSES, 1, C, 1), jnp.float32, math.log(0.5), math.log(2.0)))
    base = jnp.clip(jax.random.normal(key_base, (CLASSES, L, C, F), jnp.float32), -4.5, 4.5)
    noise = jnp.clip(jax.random.normal(key_noise, (GROUPS, CLASSES, L, C, F), jnp.float32), -4.5, 4.5)
    return (filt_scale * chan_scale * (base[None] + 0.5 * noise)).astype(jnp.float32)


def draw_consensus(key, part):
    key_scale, key_base = jax.random.split(jax.random.fold_in(key, 7), 2)
    filt_scale = jnp.exp(jax.random.uniform(key_scale, (CLASSES, 1, 1, F), jnp.float32, math.log(0.3), math.log(1.2)))
    base = jnp.clip(jax.random.normal(key_base, (CLASSES, L, C, F), jnp.float32), -4.5, 4.5)
    return (filt_scale * base).astype(jnp.float32)


def level_of(key, dims, cuts, smallest, high):
    gain = 1.0
    for position, parts in cuts:
        heights = jax.random.uniform(jax.random.fold_in(jax.random.fold_in(key, 6), position), (parts,), jnp.float32, smallest / len(cuts), high / len(cuts))
        gain = gain * jnp.repeat(jnp.exp(heights), dims[position] // parts).reshape((-1,) + (1,) * (len(dims) - 1 - position))
    return gain


def routed_block(stream_key, own, number, rows, count, top, bound, slope):
    order = jax.random.permutation(stream_key, count)
    heavy_load, ordinary = portions_of(count, rows * top, bound, slope, True), portions_of(count, rows * top, bound, slope, False)
    places = jnp.arange(count)

    def named(sizes, rotation):
        used = int((sizes > 0).sum())
        fixed = max(1, used // 4)
        shifted = fixed + (places - fixed + rotation * (used - fixed)) % max(1, count - fixed)
        return jnp.zeros((count,), jnp.int32).at[order[jnp.where(places < fixed, places, shifted)]].set(jnp.asarray(sizes, jnp.int32))

    sizes = jnp.where(number % 4 == 0, named(heavy_load, number // 4), named(ordinary, number - number // 4 - 1))
    mixed = jax.random.permutation(jax.random.fold_in(own, 3), count)
    donor, taker = mixed[0:count // 2 * 2:2], mixed[1:count // 2 * 2:2]
    room = jnp.minimum(sizes[donor] - 1, bound - sizes[taker]) // 2
    room = jnp.where((donor == order[0]) | (taker == order[0]) | (sizes[taker] == 0), 0, jnp.maximum(room, 0))
    shifted = jax.random.randint(jax.random.fold_in(own, 4), (count // 2,), 0, 1 << 20) % (room + 1)
    sizes = sizes.at[donor].add(-shifted).at[taker].add(shifted)
    items = jnp.searchsorted(jnp.cumsum(sizes), jnp.arange(rows * top), side="right").astype(jnp.int32)
    grid = items.reshape(top, rows).T
    grid = grid[jax.random.permutation(jax.random.fold_in(own, 1), rows)]
    rotation = jax.random.randint(jax.random.fold_in(own, 2), (rows, 1), 0, top)
    return jnp.take_along_axis(grid, (jnp.arange(top)[None, :] + rotation) % top, axis=1)


def portions_of(number_of, total, bound, slope, full):
    loads = [(1 << 20) // math.isqrt(standing ** slope) + 1 for standing in range(1, number_of + 1)]
    largest = bound if full else min(bound, max(-(-total // number_of), total * loads[0] // sum(loads)))
    least = 1 if total - largest >= number_of - 1 else 0
    given, rest = [largest] + [least] * (number_of - 1), total - largest - least * (number_of - 1)
    while rest > 0:
        movable = [i for i in range(1, number_of) if given[i] < largest] or [i for i in range(1, number_of) if given[i] < bound]
        mass, budget = sum([loads[i] for i in movable]), rest
        for i in movable:
            extra = min(bound - given[i], max(1, budget * loads[i] // mass), rest)
            given[i] = given[i] + extra
            rest = rest - extra
    return np.array(given)


def gaussian(key, shape, width, reach, cuts=(), kind=jnp.bfloat16):
    drawn = jax.random.normal(key, shape, jnp.float32) * width
    if len(cuts) > 0:
        drawn = level_of(key, shape, cuts, -0.22, 0.18) * drawn
    return jnp.clip(drawn, min=-reach, max=reach).astype(kind)


def setup_inputs(seed: int = 0) -> dict:
    key_list = jax.random.split(jax.random.key(seed), 8)
    signals = gaussian(key_list[0], (SIGNALS, C, T_SIZE), 1.0, 6.0, ((0, 256),), jnp.float32)
    maps = gaussian(key_list[1], (SIGNALS, USES, F, T_SIZE), (USES * F * L) ** -0.5, 0.01171875, ((0, 256),))
    uses_keys = jax.random.split(jax.random.fold_in(key_list[2], 1), SIGNALS // N_DEV)
    uses_turns = jax.random.permutation(jax.random.fold_in(key_list[2], 3), SIGNALS // N_DEV)
    uses = jax.vmap(lambda own, number: routed_block(jax.random.fold_in(key_list[2], 2), own, number, N_DEV, CLASSES, USES, READERS, 2))(uses_keys, uses_turns).reshape((SIGNALS, USES))
    owner = jax.random.permutation(key_list[3], CLASSES).astype(jnp.int32)
    local_dict = draw_local_dict(jax.random.fold_in(key_list[7], 71), 0)
    duals = gaussian(key_list[5], (GROUPS, CLASSES, L, C, F), 0.3, 4.0, ((0, 8), (1, 32)), jnp.float32)
    consensus = draw_consensus(jax.random.fold_in(key_list[7], 71), 0)
    return dict(signals=signals, maps=maps, uses=uses, owner=owner, local_dict=local_dict, duals=duals, consensus=consensus)


def shift_sum(values):
    tap_count = values.shape[0]
    time_len = values.shape[-1]
    widths = [(0, 0)] * (values.ndim - 1) + [(tap_count, 0)]
    padded = jnp.pad(values, widths)
    summed = jnp.zeros(values.shape[1:], jnp.float32)
    for lag in range(tap_count):
        summed = summed + padded[lag, ..., tap_count - lag:tap_count - lag + time_len]
    return summed

def shift_stack(source, tap_count):
    time_len = source.shape[-1]
    widths = [(0, 0)] * (source.ndim - 1) + [(0, tap_count)]
    padded = jnp.pad(source, widths)
    return jnp.stack([padded[..., lag:lag + time_len] for lag in range(tap_count)])

def project(values):
    count = values.shape[-3] * values.shape[-2]
    norms = jnp.sqrt(lax.optimization_barrier(jnp.sum(values * values, axis=(-3, -2), keepdims=True)))
    return values / jnp.maximum(1.0, norms / math.sqrt(count))
step_size = 4.0
penalty = 1.0

def reference(signals, maps, uses, owner, local_dict, duals, consensus):
    slot_of = owner[uses].astype(jnp.int32)
    group_of = (jnp.arange(signals.shape[0]) // N_DEV).astype(jnp.int32)
    dict_now = local_dict
    dual_now = duals
    cons_now = consensus
    residual = signals
    for iteration in range(ITERS):
        dict_bf = dict_now.astype(jnp.bfloat16)

        def rebuild(inputs):
            sig_maps, slots, group = inputs
            blocks = dict_bf[group, slots]
            summed = jnp.zeros((C, T_SIZE), jnp.float32)
            for entry in range(sig_maps.shape[0]):
                spread = jnp.dot(blocks[entry].reshape(L * C, F), sig_maps[entry], preferred_element_type=jnp.float32)
                summed = summed + shift_sum(spread.reshape(L, C, T_SIZE))
            return summed
        recon = lax.map(rebuild, (maps, slot_of, group_of))
        residual = signals - recon
        residual_bf = residual.astype(jnp.bfloat16)

        def accumulate(carry, inputs):
            res_one, sig_maps, slots, group = inputs
            lagged = shift_stack(res_one, L).reshape(L * C, T_SIZE)
            for entry in range(sig_maps.shape[0]):
                contrib = lax.dot_general(lagged, sig_maps[entry], (((1,), (1,)), ((), ())), preferred_element_type=jnp.float32)
                carry = carry.at[group, slots[entry]].add(contrib.reshape(L, C, F))
            return (carry, None)
        start = jnp.zeros((GROUPS, CLASSES, L, C, F), jnp.float32)
        gradient, leftover = lax.scan(accumulate, start, (residual_bf, maps, slot_of, group_of))
        new_dict = (dict_now + step_size * gradient + penalty * (cons_now[None] - dual_now)) / (1.0 + penalty)
        averaged = lax.optimization_barrier(jnp.sum(new_dict + dual_now, axis=0)) / GROUPS
        cons_new = project(averaged)
        dual_now = dual_now + new_dict - cons_new[None]
        dict_now = new_dict
        cons_now = cons_new
    return (cons_now, dual_now, residual)
```

```python
import functools

import jax
import jax.numpy as jnp
from jax import lax
from jax.experimental import pallas as pl
from jax.experimental.pallas import tpu as pltpu
from jax.sharding import PartitionSpec as P

MESH = pl.DeviceIdType.MESH
F32, BF16 = jnp.float32, jnp.bfloat16

TAPS, CHANS, FILTS, TIME = 64, 32, 256, 128
USES, DEVS, GRPS = 16, 32, 8
ZS, XS, YS = 8, 4, 4
TILE_LAGS = TAPS // GRPS
TILE = TILE_LAGS * CHANS
ROWS = TAPS * CHANS
WIDE = DEVS * TIME


def offset(step):
    place = step % ZS
    far = ZS // 2 - (place + 1) // 2
    dz = jnp.where(place % 2 == 1, far, ZS - far)
    dx = (XS - 1 - step // ZS) % XS
    return dz % ZS, dx


def kernel(
    uses_ref, owner_ref, sig_ref, maps_ref, dict_ref, dual_ref, cons_ref,
    cons_out, dual_out, res_out,
    maps_v, send_v, recv_v, dict_v, dual_v, cons_v, dictb_v, held_v, z_v, lag_v,
    sig_v, resf_v, piece_s, piece_r, res_s, res_r, sum_s, pair_r, y_s, y_r, avg_v,
    in_sem, out_sem, map_ss, map_rs, piece_ss, piece_rs, res_ss, res_rs,
    pair_ss, pair_rs, ys_ss, ys_rs, ag_ss, ag_rs, fw_ss, fw_rs,
):
    dev = lax.axis_index("dev")
    grp = lax.axis_index("grp")
    my_z, my_x = dev // XS, dev % XS
    my_y, core = grp // 2, grp % 2

    def target(step):
        dz, dx = offset(step)
        return ((my_z + dz) % ZS) * XS + (my_x + dx) % XS

    def origin(step):
        dz, dx = offset(step)
        return ((my_z + ZS - dz) % ZS) * XS + (my_x + XS - dx) % XS

    barrier = pltpu.get_barrier_semaphore()

    def greet(step, carry):
        pl.semaphore_signal(barrier, inc=1, device_id={"dev": target(step)}, device_id_type=MESH)
        return carry

    lax.fori_loop(0, DEVS - 1, greet, 0)
    for hop in range(1, YS):
        other = ((my_y + hop) % YS) * 2 + core
        pl.semaphore_signal(barrier, inc=1, device_id={"grp": other}, device_id_type=MESH)
    pl.semaphore_signal(barrier, inc=1, device_id={"grp": my_y * 2 + 1 - core}, device_id_type=MESH)

    load_maps = pltpu.make_async_copy(maps_ref.at[0], maps_v, in_sem.at[0])
    load_dict = pltpu.make_async_copy(dict_ref.at[0, 0], dict_v, in_sem.at[1])
    load_dual = pltpu.make_async_copy(dual_ref.at[0, 0], dual_v, in_sem.at[2])
    load_cons = pltpu.make_async_copy(cons_ref.at[0], cons_v, in_sem.at[3])
    load_sig = pltpu.make_async_copy(sig_ref.at[0], sig_v, in_sem.at[4])
    load_maps.start()
    load_dict.start()
    load_dual.start()
    load_cons.start()
    load_sig.start()

    slots = [owner_ref[uses_ref[0, u]] for u in range(USES)]
    load_maps.wait()
    pl.semaphore_wait(barrier, DEVS - 1 + YS)

    def block_for(d):
        at = jnp.int32(0)
        has = jnp.int32(0)
        for u in range(USES):
            hit = slots[u] == d
            at = jnp.where(hit, u, at)
            has = jnp.where(hit, 1, has)
        return maps_v[at] * has.astype(F32).astype(BF16)

    def map_copy(step, src_step, slot, to):
        return pltpu.make_async_remote_copy(
            src_ref=send_v.at[src_step],
            dst_ref=recv_v.at[slot],
            send_sem=map_ss.at[step],
            recv_sem=map_rs.at[slot],
            device_id={"dev": to},
            device_id_type=MESH,
        )

    def send_maps(step, carry):
        to = target(step)
        send_v[step] = block_for(to)
        map_copy(step, step, dev, to).start()
        return carry

    lax.fori_loop(0, DEVS - 1, send_maps, 0)
    recv_v[dev] = block_for(dev)

    load_dict.wait()

    def round_dict(tile, carry):
        rows = pl.ds(pl.multiple_of(tile * TILE, TILE), TILE)
        dictb_v[rows, :] = dict_v[pl.ds(tile * TILE_LAGS, TILE_LAGS)].reshape(TILE, FILTS).astype(BF16)
        return carry

    lax.fori_loop(0, GRPS, round_dict, 0)

    lane = lax.broadcasted_iota(jnp.int32, (CHANS, TIME), 1)

    def piece_copy(rnd, step, slot, to):
        return pltpu.make_async_remote_copy(
            src_ref=piece_s.at[rnd, step],
            dst_ref=piece_r.at[rnd, slot],
            send_sem=piece_ss.at[rnd, step],
            recv_sem=piece_rs.at[rnd, slot],
            device_id={"dev": to},
            device_id_type=MESH,
        )

    def res_copy(rnd, step, slot, to):
        return pltpu.make_async_remote_copy(
            src_ref=res_s.at[rnd],
            dst_ref=res_r.at[rnd, slot],
            send_sem=res_ss.at[rnd, step],
            recv_sem=res_rs.at[rnd, slot],
            device_id={"dev": to},
            device_id_type=MESH,
        )

    def spread(rnd):
        def pair(index, carry):
            first, second = 2 * index, 2 * index + 1
            from_first, from_second = origin(first), origin(second)
            if rnd == 0:
                map_copy(first, first, from_first, from_first).wait_recv()

                @pl.when(second < DEVS - 1)
                def _():
                    map_copy(second, second, from_second, from_second).wait_recv()

            one, two = recv_v[from_first], recv_v[from_second]
            if rnd == 0:
                held_v[pl.ds(pl.multiple_of(first * TIME, TIME), TIME), :] = one.T
                held_v[pl.ds(pl.multiple_of(second * TIME, TIME), TIME), :] = two.T
            block = jnp.concatenate([one, two], axis=1)
            total = [jnp.zeros((CHANS, TIME), F32), jnp.zeros((CHANS, TIME), F32)]
            for tile in range(GRPS):
                product = jnp.dot(
                    dictb_v[tile * TILE : (tile + 1) * TILE, :], block, preferred_element_type=F32
                )
                for near in range(TILE_LAGS):
                    lag = tile * TILE_LAGS + near
                    for half in range(2):
                        part = product[near * CHANS : (near + 1) * CHANS, half * TIME : (half + 1) * TIME]
                        if lag > 0:
                            part = jnp.where(lane >= lag, pltpu.roll(part, lag, 1), 0.0)
                        total[half] = total[half] + part
            piece_s[rnd, first] = total[0].astype(BF16)
            piece_s[rnd, second] = total[1].astype(BF16)
            piece_copy(rnd, first, dev, from_first).start()

            @pl.when(second < DEVS - 1)
            def _():
                piece_copy(rnd, second, dev, from_second).start()

            return carry

        lax.fori_loop(0, DEVS // 2, pair, 0)

    def residual(rnd):
        def add(step, total):
            slot = origin(step)
            piece_copy(rnd, step, slot, slot).wait_recv()
            return total + piece_r[rnd, slot].astype(F32)

        recon = lax.fori_loop(0, DEVS - 1, add, piece_s[rnd, DEVS - 1].astype(F32))
        left = sig_v[...] - recon
        res_s[rnd] = left.astype(BF16)

        def post(step, carry):
            res_copy(rnd, step, dev, target(step)).start()
            return carry

        lax.fori_loop(0, DEVS - 1, post, 0)
        return left

    def lagged(rnd):
        def window(back, carry):
            step = DEVS - 1 - back
            slot = origin(step)

            @pl.when(back > 0)
            def _():
                res_copy(rnd, step, slot, slot).wait_recv()
                resf_v[step] = res_r[rnd, slot].astype(F32)

            @pl.when(back == 0)
            def _():
                resf_v[step] = res_s[rnd].astype(F32)

            left = resf_v[step]
            columns = pl.ds(pl.multiple_of(step * TIME, TIME), TIME)
            for lag in range(TAPS):
                part = left
                if lag > 0:
                    part = jnp.where(lane < TIME - lag, pltpu.roll(left, TIME - lag, 1), 0.0)
                lag_v[lag * CHANS : (lag + 1) * CHANS, columns] = part.astype(BF16)
            return carry

        lax.fori_loop(0, DEVS, window, 0)

    def pair_copy(rnd, y):
        return pltpu.make_async_remote_copy(
            src_ref=sum_s.at[rnd, 2 * y + 1 - core],
            dst_ref=pair_r.at[rnd, y],
            send_sem=pair_ss.at[rnd, y],
            recv_sem=pair_rs.at[rnd, y],
            device_id={"grp": my_y * 2 + 1 - core},
            device_id_type=MESH,
        )

    def y_copy(rnd, y, slot):
        return pltpu.make_async_remote_copy(
            src_ref=y_s.at[rnd, y],
            dst_ref=y_r.at[rnd, slot],
            send_sem=ys_ss.at[rnd, y],
            recv_sem=ys_rs.at[rnd, slot],
            device_id={"grp": y * 2 + core},
            device_id_type=MESH,
        )

    def gather_copy(rnd, y, slot):
        return pltpu.make_async_remote_copy(
            src_ref=avg_v.at[rnd, slot * 2 + core],
            dst_ref=avg_v.at[rnd, slot * 2 + core],
            send_sem=ag_ss.at[rnd, y],
            recv_sem=ag_rs.at[rnd, slot],
            device_id={"grp": y * 2 + core},
            device_id_type=MESH,
        )

    def forward_copy(rnd, y, whose):
        return pltpu.make_async_remote_copy(
            src_ref=avg_v.at[rnd, y * 2 + whose],
            dst_ref=avg_v.at[rnd, y * 2 + whose],
            send_sem=fw_ss.at[rnd, y],
            recv_sem=fw_rs.at[rnd, y],
            device_id={"grp": my_y * 2 + 1 - core},
            device_id_type=MESH,
        )

    def gradient(rnd):
        def tile_step(tile, carry):
            rows = pl.ds(pl.multiple_of(tile * TILE, TILE), TILE)
            lags = pl.ds(tile * TILE_LAGS, TILE_LAGS)
            grad = jnp.dot(lag_v[rows, :], held_v[...], preferred_element_type=F32)
            grad = grad.reshape(TILE_LAGS, CHANS, FILTS)
            if rnd == 0:
                dual = dual_v[lags]
                new_dict = (dict_v[lags] + 4.0 * grad + (cons_v[lags] - dual)) * 0.5
                dict_v[lags] = new_dict
                dictb_v[rows, :] = new_dict.reshape(TILE, FILTS).astype(BF16)
                share = new_dict + dual
            else:
                share = z_v[lags] + 2.0 * grad
                z_v[lags] = share
            sum_s[rnd, tile] = share.reshape(TILE, FILTS).astype(BF16)

            @pl.when(tile % 2 != core)
            def _():
                pair_copy(rnd, tile // 2).start()

            return carry

        lax.fori_loop(0, GRPS, tile_step, 0)

    def group_pairs(rnd):
        for hop in (2, 1, 3, 0):
            y = (my_y + hop) % YS
            pair_copy(rnd, y).wait_recv()
            both = sum_s[rnd, 2 * y + core].astype(F32) + pair_r[rnd, y].astype(F32)
            y_s[rnd, y] = both.astype(BF16)
            if hop:
                y_copy(rnd, y, my_y).start()

    def group_mean(rnd):
        total = y_s[rnd, my_y].astype(F32)
        for hop in (1, 3, 2):
            y = (my_y + hop) % YS
            y_copy(rnd, y, y).wait_recv()
            total = total + y_r[rnd, y].astype(F32)
        avg_v[rnd, grp] = (total * (1.0 / GRPS)).astype(BF16)
        for hop in (2, 1, 3):
            gather_copy(rnd, (my_y + hop) % YS, my_y).start()
        forward_copy(rnd, my_y, core).start()

    def group_forward(rnd):
        for hop in (1, 3, 2):
            y = (my_y + hop) % YS
            gather_copy(rnd, y, y).wait_recv()
            forward_copy(rnd, y, core).start()

    def group_norm(rnd):
        for y in range(YS):
            forward_copy(rnd, y, 1 - core).wait_recv()

        def squares(tile, total):
            part = avg_v[rnd, tile].astype(F32)
            return total + jnp.sum((part * part).reshape(TILE // 8, 8, FILTS), axis=0)

        total = lax.fori_loop(0, GRPS, squares, jnp.zeros((8, FILTS), F32))
        norm = jnp.sqrt(jnp.sum(total, axis=0, keepdims=True))
        return 1.0 / jnp.maximum(1.0, norm * (1.0 / ROWS**0.5))

    spread(0)
    load_sig.wait()
    residual(0)
    load_dual.wait()
    load_cons.wait()
    lagged(0)
    gradient(0)
    group_pairs(0)

    spread(1)
    group_mean(0)
    left = residual(1)
    resf_v[0] = left
    store_res = pltpu.make_async_copy(resf_v.at[0], res_out.at[0], out_sem.at[2])
    store_res.start()
    store_res.wait()
    group_forward(0)
    scale = group_norm(0)

    def carry_over(tile, carry):
        lags = pl.ds(tile * TILE_LAGS, TILE_LAGS)
        cons = (avg_v[0, tile].astype(F32) * scale).reshape(TILE_LAGS, CHANS, FILTS)
        new_dict = dict_v[lags]
        dual = dual_v[lags] + new_dict - cons
        z_v[lags] = (new_dict + (cons - dual)) * 0.5 + dual
        return carry

    lax.fori_loop(0, GRPS, carry_over, 0)
    lagged(1)
    gradient(1)
    group_pairs(1)
    group_mean(1)
    group_forward(1)
    scale = group_norm(1)

    def out_copies(tile):
        lags = pl.ds(tile * TILE_LAGS, TILE_LAGS)
        return (
            pltpu.make_async_copy(cons_v.at[lags], cons_out.at[0, lags], out_sem.at[0]),
            pltpu.make_async_copy(dual_v.at[lags], dual_out.at[0, 0, lags], out_sem.at[1]),
        )

    def finish(tile, carry):
        lags = pl.ds(tile * TILE_LAGS, TILE_LAGS)
        cons = (avg_v[1, tile].astype(F32) * scale).reshape(TILE_LAGS, CHANS, FILTS)
        cons_v[lags] = cons
        dual_v[lags] = z_v[lags] - cons
        return carry

    lax.fori_loop(0, GRPS, finish, 0)
    store_cons = pltpu.make_async_copy(cons_v, cons_out.at[0], out_sem.at[0])
    store_dual = pltpu.make_async_copy(dual_v, dual_out.at[0, 0], out_sem.at[1])
    store_cons.start()
    store_dual.start()

    def sent(step, carry):
        map_copy(step, step, dev, dev).wait_send()
        for rnd in range(2):
            piece_copy(rnd, step, dev, dev).wait_send()
            res_copy(rnd, step, dev, dev).wait_send()
        return carry

    lax.fori_loop(0, DEVS - 1, sent, 0)
    for rnd in range(2):
        for y in range(YS):
            pair_copy(rnd, y).wait_send()
            forward_copy(rnd, y, core).wait_send()
        for hop in range(1, YS):
            y = (my_y + hop) % YS
            y_copy(rnd, y, my_y).wait_send()
            gather_copy(rnd, y, my_y).wait_send()
    store_cons.wait()
    store_dual.wait()


def local(signals, maps, uses, owner, local_dict, duals, consensus):
    vmem = pltpu.VMEM
    dma = pltpu.SemaphoreType.DMA
    big = (TAPS, CHANS, FILTS)
    anywhere = pl.BlockSpec(memory_space=pl.ANY)
    return pl.pallas_call(
        kernel,
        out_shape=(
            jax.ShapeDtypeStruct(consensus.shape, F32),
            jax.ShapeDtypeStruct(duals.shape, F32),
            jax.ShapeDtypeStruct(signals.shape, F32),
        ),
        in_specs=[pl.BlockSpec(memory_space=pltpu.SMEM)] * 2 + [anywhere] * 5,
        out_specs=(anywhere,) * 3,
        scratch_shapes=[
            vmem((USES, FILTS, TIME), BF16),
            vmem((DEVS, FILTS, TIME), BF16),
            vmem((DEVS, FILTS, TIME), BF16),
            vmem(big, F32),
            vmem(big, F32),
            vmem(big, F32),
            vmem((ROWS, FILTS), BF16),
            vmem((WIDE, FILTS), BF16),
            vmem(big, F32),
            vmem((ROWS, WIDE), BF16),
            vmem((CHANS, TIME), F32),
            vmem((DEVS, CHANS, TIME), F32),
            vmem((2, DEVS, CHANS, TIME), BF16),
            vmem((2, DEVS, CHANS, TIME), BF16),
            vmem((2, CHANS, TIME), BF16),
            vmem((2, DEVS, CHANS, TIME), BF16),
            vmem((2, GRPS, TILE, FILTS), BF16),
            vmem((2, YS, TILE, FILTS), BF16),
            vmem((2, YS, TILE, FILTS), BF16),
            vmem((2, YS, TILE, FILTS), BF16),
            vmem((2, GRPS, TILE, FILTS), BF16),
            dma((5,)),
            dma((3,)),
            dma((DEVS,)),
            dma((DEVS,)),
            dma((2, DEVS)),
            dma((2, DEVS)),
            dma((2, DEVS)),
            dma((2, DEVS)),
        ]
        + [dma((2, YS))] * 8,
        compiler_params=pltpu.CompilerParams(
            collective_id=0, has_side_effects=True, vmem_limit_bytes=56 * 1024 * 1024
        ),
        cost_estimate=pl.CostEstimate(flops=17_000_000_000, bytes_accessed=12_000_000, transcendentals=0),
    )(uses, owner, signals, maps, local_dict, duals, consensus)


def solution(mesh):
    placed = (
        P(("grp", "dev"), None, None),
        P(("grp", "dev"), None, None, None),
        P(("grp", "dev"), None),
        P(),
        P("grp", "dev", None, None, None),
        P("grp", "dev", None, None, None),
        P("dev", None, None, None),
    )
    return jax.shard_map(
        local,
        mesh=mesh,
        in_specs=placed,
        out_specs=(
            P("dev", None, None, None),
            P("grp", "dev", None, None, None),
            P(("grp", "dev"), None, None),
        ),
        check_vma=False,
    )
```

```python
import jax
import jax.numpy as jnp
from jax import lax
from jax.experimental import pallas as pl
from jax.experimental.pallas import tpu as pltpu
from jax.sharding import PartitionSpec as P

MESH = pl.DeviceIdType.MESH
F32, BF16 = jnp.float32, jnp.bfloat16

TAPS, CHANS, FILTS, TIME = 64, 32, 256, 128
USES, DEVS, GRPS = 16, 32, 8
ZS, XS, YS = 8, 4, 4
FINE = 8
COARSE = TAPS // FINE
TILE = COARSE * CHANS
ROWS = TAPS * CHANS
BATCH = TIME // CHANS


def offset(step):
    place = step + XS
    far = ZS // 2 - place // ZS
    dz = jnp.where(place % 2 == 1, far, ZS - far) % ZS
    dx = jnp.where(far % (ZS // 2) == 0, DEVS + XS - 1 - place, place // 2) % XS
    return dz, dx


def fixed_offset(step):
    place = step + XS
    far = ZS // 2 - place // ZS
    dz = (far if place % 2 == 1 else ZS - far) % ZS
    dx = (DEVS + XS - 1 - place if far % (ZS // 2) == 0 else place // 2) % XS
    return dz, dx


def later(values, rows):
    if rows == 0:
        return values
    return jnp.concatenate([jnp.zeros((rows, values.shape[1]), values.dtype), values[:-rows]], axis=0)


def kernel(
    uses_ref, owner_ref, sig_ref, maps_ref, dict_ref, dual_ref, cons_ref,
    cons_out, dual_out, res_out,
    maps_v, send_v, recv_v, dict_v, dual_v, cons_v, dictt_v, stage_v, mapst_v, lag_v, z_v,
    sig_v, piece_s, piece_r, res_s, res_r, left_v,
    sum_f, pair_f, sum_b, pair_b, y_s, y_r, avg_v, change_v, rest_v,
    in_sem, map_ss, map_rs, piece_ss, piece_rs, res_ss, res_rs,
    pair_ss, pair_rs, ys_ss, ys_rs, ag_ss, ag_rs, fw_ss, fw_rs,
):
    dev = lax.axis_index("dev")
    grp = lax.axis_index("grp")
    my_z, my_x = dev // XS, dev % XS
    my_y, core = grp // 2, grp % 2

    rows_of = [((my_z + dz) % ZS) * XS for dz in range(ZS)]
    columns_of = [(my_x + dx) % XS for dx in range(XS)]

    def target(step):
        dz, dx = fixed_offset(step)
        return rows_of[dz] + columns_of[dx]

    def origin(step):
        dz, dx = offset(step)
        return ((my_z + ZS - dz) % ZS) * XS + (my_x + XS - dx) % XS

    barrier = pltpu.get_barrier_semaphore()

    for step in range(DEVS - 1):
        pl.semaphore_signal(barrier, inc=1, device_id={"dev": target(step)}, device_id_type=MESH)
    for hop in range(1, YS):
        other = ((my_y + hop) % YS) * 2 + core
        pl.semaphore_signal(barrier, inc=1, device_id={"grp": other}, device_id_type=MESH)
    pl.semaphore_signal(barrier, inc=1, device_id={"grp": my_y * 2 + 1 - core}, device_id_type=MESH)

    load_maps = pltpu.make_async_copy(maps_ref.at[0], maps_v, in_sem.at[0])
    load_dict = pltpu.make_async_copy(dict_ref, dict_v, in_sem.at[1])
    load_dual = pltpu.make_async_copy(dual_ref, dual_v, in_sem.at[2])
    load_cons = pltpu.make_async_copy(cons_ref, cons_v, in_sem.at[3])
    load_sig = pltpu.make_async_copy(sig_ref.at[0], sig_v, in_sem.at[4])
    load_maps.start()
    load_dict.start()
    load_dual.start()
    load_cons.start()
    load_sig.start()

    slots = [owner_ref[uses_ref[0, u]] for u in range(USES)]
    load_maps.wait()

    def block_for(d):
        at = jnp.int32(0)
        has = jnp.int32(0)
        for u in range(USES):
            hit = slots[u] == d
            at = jnp.where(hit, u, at)
            has = jnp.where(hit, 1, has)
        return maps_v[at] * has.astype(F32).astype(BF16)

    def map_copy(step, to):
        return pltpu.make_async_remote_copy(
            src_ref=send_v.at[step],
            dst_ref=recv_v.at[step],
            send_sem=map_ss.at[step],
            recv_sem=map_rs.at[step],
            device_id={"dev": to},
            device_id_type=MESH,
        )

    pl.semaphore_wait(barrier, DEVS - 1 + YS)
    for step in range(DEVS - 1):
        send_v[step] = block_for(target(step))
        map_copy(step, target(step)).start()
    recv_v[DEVS - 1] = block_for(dev)

    load_dict.wait()

    def turned(tile):
        return tile.reshape(TILE, FILTS).astype(BF16).T

    def turn_dict(tile, carry):
        dictt_v[pl.ds(pl.multiple_of(tile * FILTS, FILTS), FILTS), :] = turned(dict_v[:, tile])
        return carry

    lax.fori_loop(0, FINE, turn_dict, 0)
    for place in range(BATCH):
        stage_v[place, :FINE, :] = jnp.zeros((FINE, FILTS), F32)

    lane_t = lax.broadcasted_iota(jnp.int32, (CHANS, TIME), 1)
    lane_part = lax.broadcasted_iota(jnp.int32, (TIME, TIME), 1) // CHANS

    def piece_copy(rnd, step, to):
        return pltpu.make_async_remote_copy(
            src_ref=piece_s.at[rnd, step],
            dst_ref=piece_r.at[rnd, step],
            send_sem=piece_ss.at[rnd, step],
            recv_sem=piece_rs.at[rnd, step],
            device_id={"dev": to},
            device_id_type=MESH,
        )

    def res_copy(rnd, step, to):
        return pltpu.make_async_remote_copy(
            src_ref=res_s.at[rnd],
            dst_ref=res_r.at[rnd, step],
            send_sem=res_ss.at[rnd, step],
            recv_sem=res_rs.at[rnd, step],
            device_id={"dev": to},
            device_id_type=MESH,
        )

    def fold(product):
        half = product[:, :TIME] + later(product[:, TIME:], BATCH * FINE)
        mixed = half
        for part in range(1, BATCH):
            mixed = jnp.where(lane_part == part, later(half, part * FINE), mixed)
        mixed = mixed + pltpu.roll(mixed, 2 * CHANS, 1)
        return mixed + pltpu.roll(mixed, CHANS, 1)

    def spread(rnd, low, high):
        def batch(index, carry):
            first = index * BATCH
            if rnd == 0:
                for place in range(BATCH):
                    step = first + place
                    if place == BATCH - 1:

                        @pl.when(step < DEVS - 1)
                        def _():
                            map_copy(step, origin(step)).wait_recv()

                    else:
                        map_copy(step, origin(step)).wait_recv()
                for place in range(BATCH):
                    step = first + place
                    stage_v[place, FINE:, :] = recv_v[step].T.astype(F32)
                    for fine in range(FINE):
                        mapst_v[step, :, fine * FILTS : (fine + 1) * FILTS] = stage_v[
                            place, FINE - fine : FINE - fine + TIME, :
                        ].astype(BF16)
            held = mapst_v[pl.ds(first, BATCH)].reshape(BATCH * TIME, FINE * FILTS)
            product = jnp.dot(held, dictt_v[...], preferred_element_type=F32)
            gathered = fold(product[:TIME])
            for place in range(1, BATCH):
                one = fold(product[place * TIME : (place + 1) * TIME])
                gathered = jnp.where(lane_part == place, one, gathered)
            pieces = gathered.T.astype(BF16)
            for place in range(BATCH):
                piece_s[rnd, first + place] = pieces[place * CHANS : (place + 1) * CHANS]
            for place in range(BATCH):
                step = first + place
                if place == BATCH - 1:

                    @pl.when(step < DEVS - 1)
                    def _():
                        piece_copy(rnd, step, origin(step)).start()

                else:
                    piece_copy(rnd, step, origin(step)).start()
            return carry

        lax.fori_loop(low, high, batch, 0)

    def residual(rnd):
        for step in range(DEVS - 1):
            piece_copy(rnd, step, target(step)).wait_recv()
        parts = [piece_r[rnd, step].astype(F32) for step in range(DEVS - 1)]
        parts.append(piece_s[rnd, DEVS - 1].astype(F32))
        while len(parts) > 1:
            parts = [one + two for one, two in zip(parts[::2], parts[1::2], strict=True)]
        recon = parts[0]
        left = sig_v[...] - recon
        res_s[rnd] = left.astype(BF16)
        left_v[DEVS - 1] = left.astype(BF16).astype(F32)

        for step in range(DEVS - 1):
            res_copy(rnd, step, target(step)).start()
        return left

    def lagged(rnd):
        for step in range(DEVS - 1):
            res_copy(rnd, step, target(step)).wait_recv()
            left_v[step] = res_r[rnd, step].astype(F32)

        def some(index, carry):
            for place in range(BATCH):
                step = index * BATCH + place
                left = left_v[step]
                columns = pl.ds(pl.multiple_of(step * TIME, TIME), TIME)
                for coarse in range(COARSE):
                    lag = coarse * FINE
                    part = left
                    if lag > 0:
                        part = jnp.where(lane_t < TIME - lag, pltpu.roll(left, TIME - lag, 1), 0.0)
                    lag_v[coarse * CHANS : (coarse + 1) * CHANS, columns] = part.astype(BF16)
            return carry

        lax.fori_loop(0, DEVS // BATCH, some, 0)

    def pair_copy(rnd, y):
        sums, pairs = ((sum_f, pair_f), (sum_b, pair_b))[rnd]
        return pltpu.make_async_remote_copy(
            src_ref=sums.at[2 * y + 1 - core],
            dst_ref=pairs.at[y],
            send_sem=pair_ss.at[rnd, y],
            recv_sem=pair_rs.at[rnd, y],
            device_id={"grp": my_y * 2 + 1 - core},
            device_id_type=MESH,
        )

    def y_copy(rnd, y, slot):
        return pltpu.make_async_remote_copy(
            src_ref=y_s.at[rnd, y],
            dst_ref=y_r.at[rnd, slot],
            send_sem=ys_ss.at[rnd, y],
            recv_sem=ys_rs.at[rnd, slot],
            device_id={"grp": y * 2 + core},
            device_id_type=MESH,
        )

    means = (avg_v, change_v, rest_v)

    def gather_copy(kind, y, slot):
        where = means[kind].at[slot * 2 + core]
        return pltpu.make_async_remote_copy(
            src_ref=where,
            dst_ref=where,
            send_sem=ag_ss.at[kind, y],
            recv_sem=ag_rs.at[kind, slot],
            device_id={"grp": y * 2 + core},
            device_id_type=MESH,
        )

    def forward_copy(kind, y, whose):
        where = means[kind].at[y * 2 + whose]
        return pltpu.make_async_remote_copy(
            src_ref=where,
            dst_ref=where,
            send_sem=fw_ss.at[kind, y],
            recv_sem=fw_rs.at[kind, y],
            device_id={"grp": my_y * 2 + 1 - core},
            device_id_type=MESH,
        )

    def gradient(rnd):
        sums, pairs = ((sum_f, pair_f), (sum_b, pair_b))[rnd]

        def one_tile(tile):
            wide = pl.ds(pl.multiple_of(tile * FILTS, FILTS), FILTS)
            held = mapst_v[:, :, wide].reshape(DEVS * TIME, FILTS)
            grad = jnp.dot(lag_v[...], held, preferred_element_type=F32)
            if rnd == 0:
                grad = grad.reshape(COARSE, CHANS, FILTS)
                dual = dual_v[:, tile]
                new_dict = (dict_v[:, tile] + 4.0 * grad + (cons_v[:, tile] - dual)) * 0.5
                dict_v[:, tile] = new_dict
                dictt_v[wide, :] = turned(new_dict)
                sum_f[tile] = (new_dict + dual).reshape(TILE, FILTS)
            else:
                both = z_v[tile] + 2.0 * grad
                z_v[tile] = both
                sum_b[tile] = (both - sum_f[tile]).astype(BF16)

        def add_pair(y):
            pair_copy(rnd, y).wait_recv()
            both = sums[2 * y + core].astype(F32) + pairs[y].astype(F32)
            y_s[rnd, y] = both.astype(BF16)

        def two_tiles(y):
            one_tile(2 * y + 1 - core)
            pair_copy(rnd, y).start()
            one_tile(2 * y + core)
            add_pair(y)

        def away(turn, carry):
            y = (my_y + 1 + turn) % YS
            two_tiles(y)
            y_copy(rnd, y, my_y).start()
            return carry

        lax.fori_loop(0, YS - 1, away, 0)
        two_tiles(my_y)

    def group_mean(rnd):
        total = y_s[rnd, my_y].astype(F32)
        for hop in (1, 3, 2):
            y = (my_y + hop) % YS
            y_copy(rnd, y, y).wait_recv()
            total = total + y_r[rnd, y].astype(F32)
        total = total * (1.0 / GRPS)
        kinds = (0, 2) if rnd == 0 else (1,)
        for kind in kinds:
            short = total.astype(BF16)
            means[kind][grp] = short
            total = total - short.astype(F32)
            for hop in (2, 1, 3):
                gather_copy(kind, (my_y + hop) % YS, my_y).start()
            forward_copy(kind, my_y, core).start()

    def group_forward(kind):
        for hop in (1, 3, 2):
            y = (my_y + hop) % YS
            gather_copy(kind, y, y).wait_recv()
            forward_copy(kind, y, core).start()

    def group_close(kind):
        for y in range(YS):
            forward_copy(kind, y, 1 - core).wait_recv()

    def mean_of(rnd, tile):
        mean = avg_v[tile].astype(F32)
        if rnd == 1:
            mean = mean + rest_v[tile].astype(F32) + change_v[tile].astype(F32)
        return mean

    def scale_of(rnd):
        def squares(tile, total):
            part = mean_of(rnd, tile)
            return total + jnp.sum((part * part).reshape(TILE // 8, 8, FILTS), axis=0)

        total = lax.fori_loop(0, FINE, squares, jnp.zeros((8, FILTS), F32))
        norm = jnp.sqrt(jnp.sum(total, axis=0, keepdims=True))
        return 1.0 / jnp.maximum(1.0, norm * (1.0 / ROWS**0.5))

    batches = DEVS // BATCH

    spread(0, 0, batches)
    load_sig.wait()
    residual(0)
    load_dual.wait()
    load_cons.wait()
    lagged(0)
    gradient(0)

    spread(1, 0, batches // 2)
    group_mean(0)
    spread(1, batches // 2, batches)
    res_out[0] = residual(1)
    group_forward(0)
    group_close(0)
    scale = scale_of(0)

    def carry_over(tile, carry):
        cons = (mean_of(0, tile) * scale).reshape(COARSE, CHANS, FILTS)
        new_dict = dict_v[:, tile]
        dual = dual_v[:, tile] + new_dict - cons
        z_v[tile] = ((new_dict + (cons - dual)) * 0.5 + dual).reshape(TILE, FILTS)
        return carry

    lax.fori_loop(0, FINE, carry_over, 0)
    lagged(1)
    gradient(1)
    group_forward(2)
    group_mean(1)
    group_close(2)
    group_forward(1)
    group_close(1)
    scale_end = scale_of(1)

    def finish(tile, carry):
        cons = mean_of(1, tile) * scale_end
        cons_out[:, tile] = cons.reshape(COARSE, CHANS, FILTS)
        dual_out[:, tile] = (z_v[tile] - cons).reshape(COARSE, CHANS, FILTS)
        return carry

    lax.fori_loop(0, FINE, finish, 0)

    for step in range(DEVS - 1):
        map_copy(step, target(step)).wait_send()
        for rnd in range(2):
            piece_copy(rnd, step, target(step)).wait_send()
            res_copy(rnd, step, target(step)).wait_send()
    for rnd in range(2):
        for y in range(YS):
            pair_copy(rnd, y).wait_send()
        for hop in range(1, YS):
            y_copy(rnd, (my_y + hop) % YS, my_y).wait_send()
    for kind in range(3):
        for y in range(YS):
            forward_copy(kind, y, core).wait_send()
        for hop in range(1, YS):
            gather_copy(kind, (my_y + hop) % YS, my_y).wait_send()


def local(signals, maps, uses, owner, local_dict, duals, consensus):
    vmem = pltpu.VMEM
    dma = pltpu.SemaphoreType.DMA
    split = (COARSE, FINE, CHANS, FILTS)
    tiles = (FINE, TILE, FILTS)
    quarter = (YS, TILE, FILTS)
    cons_new, dual_new, left = pl.pallas_call(
        kernel,
        out_shape=(
            jax.ShapeDtypeStruct(split, F32),
            jax.ShapeDtypeStruct(split, F32),
            jax.ShapeDtypeStruct(signals.shape, F32),
        ),
        in_specs=[pl.BlockSpec(memory_space=pltpu.SMEM)] * 2 + [pl.BlockSpec(memory_space=pltpu.HBM)] * 5,
        out_specs=(pl.BlockSpec(memory_space=pltpu.VMEM),) * 3,
        scratch_shapes=[
            vmem((USES, FILTS, TIME), BF16),
            vmem((DEVS, FILTS, TIME), BF16),
            vmem((DEVS, FILTS, TIME), BF16),
            vmem(split, F32),
            vmem(split, F32),
            vmem(split, F32),
            vmem((FINE * FILTS, TILE), BF16),
            vmem((BATCH, FINE + TIME, FILTS), F32),
            vmem((DEVS, TIME, FINE * FILTS), BF16),
            vmem((TILE, DEVS * TIME), BF16),
            vmem(tiles, F32),
            vmem((CHANS, TIME), F32),
            vmem((2, DEVS, CHANS, TIME), BF16),
            vmem((2, DEVS, CHANS, TIME), BF16),
            vmem((2, CHANS, TIME), BF16),
            vmem((2, DEVS, CHANS, TIME), BF16),
            vmem((DEVS, CHANS, TIME), F32),
            vmem(tiles, F32),
            vmem(quarter, F32),
            vmem(tiles, BF16),
            vmem(quarter, BF16),
            vmem((2,) + quarter, BF16),
            vmem((2,) + quarter, BF16),
            vmem(tiles, BF16),
            vmem(tiles, BF16),
            vmem(tiles, BF16),
            dma((5,)),
            dma((DEVS,)),
            dma((DEVS,)),
            dma((2, DEVS)),
            dma((2, DEVS)),
            dma((2, DEVS)),
            dma((2, DEVS)),
        ]
        + [dma((2, YS))] * 4
        + [dma((3, YS))] * 4,
        compiler_params=pltpu.CompilerParams(
            collective_id=0, has_side_effects=True, vmem_limit_bytes=48 * 1024 * 1024
        ),
        cost_estimate=pl.CostEstimate(flops=17_000_000_000, bytes_accessed=12_000_000, transcendentals=0),
    )(uses, owner, signals, maps, local_dict.reshape(split), duals.reshape(split), consensus.reshape(split))
    return cons_new.reshape(consensus.shape), dual_new.reshape(duals.shape), left


def solution(mesh):
    placed = (
        P(("grp", "dev"), None, None),
        P(("grp", "dev"), None, None, None),
        P(("grp", "dev"), None),
        P(),
        P("grp", "dev", None, None, None),
        P("grp", "dev", None, None, None),
        P("dev", None, None, None),
    )
    return jax.shard_map(
        local,
        mesh=mesh,
        in_specs=placed,
        out_specs=(
            P("dev", None, None, None),
            P("grp", "dev", None, None, None),
            P(("grp", "dev"), None, None),
        ),
        check_vma=False,
    )
```

```python
import jax
import jax.numpy as jnp
from jax import lax
from jax.experimental import pallas as pl
from jax.experimental.pallas import tpu as pltpu
from jax.sharding import PartitionSpec as P

MESH = pl.DeviceIdType.MESH
F32, BF16 = jnp.float32, jnp.bfloat16

TAPS, CHANS, FILTS, TIME = 64, 32, 256, 128
USES, DEVS, GRPS = 16, 32, 8
ZS, XS, YS = 8, 4, 4
FINE = 8
COARSE = TAPS // FINE
TILE = COARSE * CHANS
ROWS = TAPS * CHANS
BATCH = TIME // CHANS


def offset(step):
    place = step + XS
    far = ZS // 2 - place // ZS
    dz = jnp.where(place % 2 == 1, far, ZS - far) % ZS
    dx = jnp.where(far % (ZS // 2) == 0, DEVS + XS - 1 - place, place // 2) % XS
    return dz, dx


def fixed_offset(step):
    place = step + XS
    far = ZS // 2 - place // ZS
    dz = (far if place % 2 == 1 else ZS - far) % ZS
    dx = (DEVS + XS - 1 - place if far % (ZS // 2) == 0 else place // 2) % XS
    return dz, dx


def later(values, rows):
    if rows == 0:
        return values
    return jnp.concatenate([jnp.zeros((rows, values.shape[1]), values.dtype), values[:-rows]], axis=0)


def kernel(
    uses_ref, owner_ref, sig_ref, maps_ref, dict_ref, dual_ref, cons_ref,
    cons_out, dual_out, res_out,
    maps_v, send_v, recv_v, dict_v, dual_v, cons_v, dictt_v, stage_v, mapst_v, lag_v, z_v,
    sig_v, piece_s, piece_r, res_s, res_r, left_v,
    sum_f, pair_f, sum_b, pair_b, y_s, y_r, avg_v, change_v, rest_v,
    in_sem, map_ss, map_rs, piece_ss, piece_rs, res_ss, res_rs,
    pair_ss, pair_rs, ys_ss, ys_rs, ag_ss, ag_rs, fw_ss, fw_rs,
):
    dev = lax.axis_index("dev")
    grp = lax.axis_index("grp")
    my_z, my_x = dev // XS, dev % XS
    my_y, core = grp // 2, grp % 2

    rows_of = [((my_z + dz) % ZS) * XS for dz in range(ZS)]
    columns_of = [(my_x + dx) % XS for dx in range(XS)]

    def target(step):
        dz, dx = fixed_offset(step)
        return rows_of[dz] + columns_of[dx]

    def origin(step):
        dz, dx = offset(step)
        return ((my_z + ZS - dz) % ZS) * XS + (my_x + XS - dx) % XS

    barrier = pltpu.get_barrier_semaphore()

    for step in range(DEVS - 1):
        pl.semaphore_signal(barrier, inc=1, device_id={"dev": target(step)}, device_id_type=MESH)
    for hop in range(1, YS):
        other = ((my_y + hop) % YS) * 2 + core
        pl.semaphore_signal(barrier, inc=1, device_id={"grp": other}, device_id_type=MESH)
    pl.semaphore_signal(barrier, inc=1, device_id={"grp": my_y * 2 + 1 - core}, device_id_type=MESH)

    load_maps = pltpu.make_async_copy(maps_ref.at[0], maps_v, in_sem.at[0])
    load_dict = pltpu.make_async_copy(dict_ref, dict_v, in_sem.at[1])
    load_dual = pltpu.make_async_copy(dual_ref, dual_v, in_sem.at[2])
    load_cons = pltpu.make_async_copy(cons_ref, cons_v, in_sem.at[3])
    load_sig = pltpu.make_async_copy(sig_ref.at[0], sig_v, in_sem.at[4])
    load_maps.start()
    load_dict.start()
    load_dual.start()
    load_cons.start()
    load_sig.start()

    slots = [owner_ref[uses_ref[0, u]] for u in range(USES)]
    load_maps.wait()

    def block_for(d):
        at = jnp.int32(0)
        has = jnp.int32(0)
        for u in range(USES):
            hit = slots[u] == d
            at = jnp.where(hit, u, at)
            has = jnp.where(hit, 1, has)
        return maps_v[at] * has.astype(F32).astype(BF16)

    def map_copy(step, to):
        return pltpu.make_async_remote_copy(
            src_ref=send_v.at[step],
            dst_ref=recv_v.at[step],
            send_sem=map_ss.at[step],
            recv_sem=map_rs.at[step],
            device_id={"dev": to},
            device_id_type=MESH,
        )

    pl.semaphore_wait(barrier, DEVS - 1 + YS)
    for step in range(DEVS - 1):
        send_v[step] = block_for(target(step))
        map_copy(step, target(step)).start()
    recv_v[DEVS - 1] = block_for(dev)

    load_dict.wait()

    def turned(tile):
        return tile.reshape(TILE, FILTS).astype(BF16).T

    def turn_dict(tile, carry):
        dictt_v[pl.ds(pl.multiple_of(tile * FILTS, FILTS), FILTS), :] = turned(dict_v[:, tile])
        return carry

    lax.fori_loop(0, FINE, turn_dict, 0)
    for place in range(BATCH):
        stage_v[place, :FINE, :] = jnp.zeros((FINE, FILTS), F32)

    lane_t = lax.broadcasted_iota(jnp.int32, (CHANS, TIME), 1)
    lane_part = lax.broadcasted_iota(jnp.int32, (TIME, TIME), 1) // CHANS

    def piece_copy(rnd, step, to):
        return pltpu.make_async_remote_copy(
            src_ref=piece_s.at[rnd, step],
            dst_ref=piece_r.at[rnd, step],
            send_sem=piece_ss.at[rnd, step],
            recv_sem=piece_rs.at[rnd, step],
            device_id={"dev": to},
            device_id_type=MESH,
        )

    def res_copy(rnd, step, to):
        return pltpu.make_async_remote_copy(
            src_ref=res_s.at[rnd],
            dst_ref=res_r.at[rnd, step],
            send_sem=res_ss.at[rnd, step],
            recv_sem=res_rs.at[rnd, step],
            device_id={"dev": to},
            device_id_type=MESH,
        )

    def fold(product):
        half = product[:, :TIME] + later(product[:, TIME:], BATCH * FINE)
        mixed = half
        for part in range(1, BATCH):
            mixed = jnp.where(lane_part == part, later(half, part * FINE), mixed)
        mixed = mixed + pltpu.roll(mixed, 2 * CHANS, 1)
        return mixed + pltpu.roll(mixed, CHANS, 1)

    def spread(rnd, low, high):
        def batch(index, carry):
            first = index * BATCH
            if rnd == 0:
                for place in range(BATCH):
                    step = first + place
                    if place == BATCH - 1:

                        @pl.when(step < DEVS - 1)
                        def _():
                            map_copy(step, origin(step)).wait_recv()

                    else:
                        map_copy(step, origin(step)).wait_recv()
                for place in range(BATCH):
                    step = first + place
                    stage_v[place, FINE:, :] = recv_v[step].T.astype(F32)
                    for fine in range(FINE):
                        mapst_v[step, :, fine * FILTS : (fine + 1) * FILTS] = stage_v[
                            place, FINE - fine : FINE - fine + TIME, :
                        ].astype(BF16)
            held = mapst_v[pl.ds(first, BATCH)].reshape(BATCH * TIME, FINE * FILTS)
            product = jnp.dot(held, dictt_v[...], preferred_element_type=F32)
            gathered = fold(product[:TIME])
            for place in range(1, BATCH):
                one = fold(product[place * TIME : (place + 1) * TIME])
                gathered = jnp.where(lane_part == place, one, gathered)
            pieces = gathered.T.astype(BF16)
            for place in range(BATCH):
                piece_s[rnd, first + place] = pieces[place * CHANS : (place + 1) * CHANS]
            for place in range(BATCH):
                step = first + place
                if place == BATCH - 1:

                    @pl.when(step < DEVS - 1)
                    def _():
                        piece_copy(rnd, step, origin(step)).start()

                else:
                    piece_copy(rnd, step, origin(step)).start()
            return carry

        lax.fori_loop(low, high, batch, 0)

    def residual(rnd):
        for step in range(DEVS - 1):
            piece_copy(rnd, step, target(step)).wait_recv()
        parts = [piece_r[rnd, step].astype(F32) for step in range(DEVS - 1)]
        parts.append(piece_s[rnd, DEVS - 1].astype(F32))
        while len(parts) > 1:
            parts = [one + two for one, two in zip(parts[::2], parts[1::2], strict=True)]
        recon = parts[0]
        left = sig_v[...] - recon
        res_s[rnd] = left.astype(BF16)
        left_v[DEVS - 1] = left.astype(BF16).astype(F32)

        for step in range(DEVS - 1):
            res_copy(rnd, step, target(step)).start()
        return left

    def lagged(rnd):
        for step in range(DEVS - 1):
            res_copy(rnd, step, target(step)).wait_recv()
            left_v[step] = res_r[rnd, step].astype(F32)

        def some(index, carry):
            for place in range(BATCH):
                step = index * BATCH + place
                left = left_v[step]
                columns = pl.ds(pl.multiple_of(step * TIME, TIME), TIME)
                for coarse in range(COARSE):
                    lag = coarse * FINE
                    part = left
                    if lag > 0:
                        part = jnp.where(lane_t < TIME - lag, pltpu.roll(left, TIME - lag, 1), 0.0)
                    lag_v[coarse * CHANS : (coarse + 1) * CHANS, columns] = part.astype(BF16)
            return carry

        lax.fori_loop(0, DEVS // BATCH, some, 0)

    def pair_copy(rnd, y):
        sums, pairs = ((sum_f, pair_f), (sum_b, pair_b))[rnd]
        return pltpu.make_async_remote_copy(
            src_ref=sums.at[2 * y + 1 - core],
            dst_ref=pairs.at[y],
            send_sem=pair_ss.at[rnd, y],
            recv_sem=pair_rs.at[rnd, y],
            device_id={"grp": my_y * 2 + 1 - core},
            device_id_type=MESH,
        )

    def y_copy(rnd, y, slot):
        return pltpu.make_async_remote_copy(
            src_ref=y_s.at[rnd, y],
            dst_ref=y_r.at[rnd, slot],
            send_sem=ys_ss.at[rnd, y],
            recv_sem=ys_rs.at[rnd, slot],
            device_id={"grp": y * 2 + core},
            device_id_type=MESH,
        )

    means = (avg_v, change_v, rest_v)

    def gather_copy(kind, y, slot):
        where = means[kind].at[slot * 2 + core]
        return pltpu.make_async_remote_copy(
            src_ref=where,
            dst_ref=where,
            send_sem=ag_ss.at[kind, y],
            recv_sem=ag_rs.at[kind, slot],
            device_id={"grp": y * 2 + core},
            device_id_type=MESH,
        )

    def forward_copy(kind, y, whose):
        where = means[kind].at[y * 2 + whose]
        return pltpu.make_async_remote_copy(
            src_ref=where,
            dst_ref=where,
            send_sem=fw_ss.at[kind, y],
            recv_sem=fw_rs.at[kind, y],
            device_id={"grp": my_y * 2 + 1 - core},
            device_id_type=MESH,
        )

    def gradient(rnd):
        sums, pairs = ((sum_f, pair_f), (sum_b, pair_b))[rnd]

        def one_tile(tile):
            wide = pl.ds(pl.multiple_of(tile * FILTS, FILTS), FILTS)
            held = mapst_v[:, :, wide].reshape(DEVS * TIME, FILTS)
            grad = jnp.dot(lag_v[...], held, preferred_element_type=F32)
            if rnd == 0:
                grad = grad.reshape(COARSE, CHANS, FILTS)
                dual = dual_v[:, tile]
                new_dict = (dict_v[:, tile] + 4.0 * grad + (cons_v[:, tile] - dual)) * 0.5
                dict_v[:, tile] = new_dict
                dictt_v[wide, :] = turned(new_dict)
                sum_f[tile] = (new_dict + dual).reshape(TILE, FILTS)
            else:
                both = z_v[tile] + 2.0 * grad
                z_v[tile] = both
                sum_b[tile] = (both - sum_f[tile]).astype(BF16)

        def add_pair(y):
            pair_copy(rnd, y).wait_recv()
            both = sums[2 * y + core].astype(F32) + pairs[y].astype(F32)
            y_s[rnd, y] = both.astype(BF16)

        def two_tiles(y):
            one_tile(2 * y + 1 - core)
            pair_copy(rnd, y).start()
            one_tile(2 * y + core)
            add_pair(y)

        def away(turn, carry):
            y = (my_y + 1 + turn) % YS
            two_tiles(y)
            y_copy(rnd, y, my_y).start()
            return carry

        lax.fori_loop(0, YS - 1, away, 0)
        two_tiles(my_y)

    def group_mean(rnd):
        total = y_s[rnd, my_y].astype(F32)
        for hop in (1, 3, 2):
            y = (my_y + hop) % YS
            y_copy(rnd, y, y).wait_recv()
            total = total + y_r[rnd, y].astype(F32)
        total = total * (1.0 / GRPS)
        kinds = (0, 2) if rnd == 0 else (1,)
        for kind in kinds:
            short = total.astype(BF16)
            means[kind][grp] = short
            total = total - short.astype(F32)
            for hop in (2, 1, 3):
                gather_copy(kind, (my_y + hop) % YS, my_y).start()
            forward_copy(kind, my_y, core).start()

    def group_forward(kind):
        for hop in (1, 3, 2):
            y = (my_y + hop) % YS
            gather_copy(kind, y, y).wait_recv()
            forward_copy(kind, y, core).start()

    def group_close(kind):
        for y in range(YS):
            forward_copy(kind, y, 1 - core).wait_recv()

    def mean_of(rnd, tile):
        mean = avg_v[tile].astype(F32)
        if rnd == 1:
            mean = mean + rest_v[tile].astype(F32) + change_v[tile].astype(F32)
        return mean

    def scale_of(rnd):
        def squares(tile, total):
            part = mean_of(rnd, tile)
            return total + jnp.sum((part * part).reshape(TILE // 8, 8, FILTS), axis=0)

        total = lax.fori_loop(0, FINE, squares, jnp.zeros((8, FILTS), F32))
        norm = jnp.sqrt(jnp.sum(total, axis=0, keepdims=True))
        return 1.0 / jnp.maximum(1.0, norm * (1.0 / ROWS**0.5))

    batches = DEVS // BATCH

    spread(0, 0, batches)
    load_sig.wait()
    residual(0)
    load_dual.wait()
    load_cons.wait()
    lagged(0)
    gradient(0)

    spread(1, 0, batches)
    group_mean(0)
    res_out[0] = residual(1)
    group_forward(0)
    group_close(0)
    scale = scale_of(0)

    def carry_over(tile, carry):
        cons = (mean_of(0, tile) * scale).reshape(COARSE, CHANS, FILTS)
        new_dict = dict_v[:, tile]
        dual = dual_v[:, tile] + new_dict - cons
        z_v[tile] = ((new_dict + (cons - dual)) * 0.5 + dual).reshape(TILE, FILTS)
        return carry

    lax.fori_loop(0, FINE, carry_over, 0)
    lagged(1)
    gradient(1)
    group_forward(2)
    group_mean(1)
    group_close(2)
    group_forward(1)
    group_close(1)
    scale_end = scale_of(1)

    def finish(tile, carry):
        cons = mean_of(1, tile) * scale_end
        cons_out[:, tile] = cons.reshape(COARSE, CHANS, FILTS)
        dual_out[:, tile] = (z_v[tile] - cons).reshape(COARSE, CHANS, FILTS)
        return carry

    lax.fori_loop(0, FINE, finish, 0)

    for step in range(DEVS - 1):
        map_copy(step, target(step)).wait_send()
        for rnd in range(2):
            piece_copy(rnd, step, target(step)).wait_send()
            res_copy(rnd, step, target(step)).wait_send()
    for rnd in range(2):
        for y in range(YS):
            pair_copy(rnd, y).wait_send()
        for hop in range(1, YS):
            y_copy(rnd, (my_y + hop) % YS, my_y).wait_send()
    for kind in range(3):
        for y in range(YS):
            forward_copy(kind, y, core).wait_send()
        for hop in range(1, YS):
            gather_copy(kind, (my_y + hop) % YS, my_y).wait_send()


def local(signals, maps, uses, owner, local_dict, duals, consensus):
    vmem = pltpu.VMEM
    dma = pltpu.SemaphoreType.DMA
    split = (COARSE, FINE, CHANS, FILTS)
    tiles = (FINE, TILE, FILTS)
    quarter = (YS, TILE, FILTS)
    cons_new, dual_new, left = pl.pallas_call(
        kernel,
        out_shape=(
            jax.ShapeDtypeStruct(split, F32),
            jax.ShapeDtypeStruct(split, F32),
            jax.ShapeDtypeStruct(signals.shape, F32),
        ),
        in_specs=[pl.BlockSpec(memory_space=pltpu.SMEM)] * 2 + [pl.BlockSpec(memory_space=pltpu.HBM)] * 5,
        out_specs=(pl.BlockSpec(memory_space=pltpu.VMEM),) * 3,
        scratch_shapes=[
            vmem((USES, FILTS, TIME), BF16),
            vmem((DEVS, FILTS, TIME), BF16),
            vmem((DEVS, FILTS, TIME), BF16),
            vmem(split, F32),
            vmem(split, F32),
            vmem(split, F32),
            vmem((FINE * FILTS, TILE), BF16),
            vmem((BATCH, FINE + TIME, FILTS), F32),
            vmem((DEVS, TIME, FINE * FILTS), BF16),
            vmem((TILE, DEVS * TIME), BF16),
            vmem(tiles, F32),
            vmem((CHANS, TIME), F32),
            vmem((2, DEVS, CHANS, TIME), BF16),
            vmem((2, DEVS, CHANS, TIME), BF16),
            vmem((2, CHANS, TIME), BF16),
            vmem((2, DEVS, CHANS, TIME), BF16),
            vmem((DEVS, CHANS, TIME), F32),
            vmem(tiles, F32),
            vmem(quarter, F32),
            vmem(tiles, BF16),
            vmem(quarter, BF16),
            vmem((2,) + quarter, BF16),
            vmem((2,) + quarter, BF16),
            vmem(tiles, BF16),
            vmem(tiles, BF16),
            vmem(tiles, BF16),
            dma((5,)),
            dma((DEVS,)),
            dma((DEVS,)),
            dma((2, DEVS)),
            dma((2, DEVS)),
            dma((2, DEVS)),
            dma((2, DEVS)),
        ]
        + [dma((2, YS))] * 4
        + [dma((3, YS))] * 4,
        compiler_params=pltpu.CompilerParams(
            collective_id=0, has_side_effects=True, vmem_limit_bytes=48 * 1024 * 1024
        ),
        cost_estimate=pl.CostEstimate(flops=17_000_000_000, bytes_accessed=12_000_000, transcendentals=0),
    )(uses, owner, signals, maps, local_dict.reshape(split), duals.reshape(split), consensus.reshape(split))
    return cons_new.reshape(consensus.shape), dual_new.reshape(duals.shape), left


def solution(mesh):
    placed = (
        P(("grp", "dev"), None, None),
        P(("grp", "dev"), None, None, None),
        P(("grp", "dev"), None),
        P(),
        P("grp", "dev", None, None, None),
        P("grp", "dev", None, None, None),
        P("dev", None, None, None),
    )
    return jax.shard_map(
        local,
        mesh=mesh,
        in_specs=placed,
        out_specs=(
            P("dev", None, None, None),
            P("grp", "dev", None, None, None),
            P(("grp", "dev"), None, None),
        ),
        check_vma=False,
    )
```
